768 devices in a mesh: seq: 192 (over z, x, y_lo), head: 4 (over y_hi, core).
Axes of the slice: x: 4, y: 8 (y_hi: 2, y_lo: 4; y = y_hi * 4 + y_lo), z: 12, core: 2. Of those that a mesh axis runs over, the one named last changes fastest.
Arguments:
- tokens: bfloat16 [98304, 2048], P('seq', 'head')
- w_query: bfloat16 [2048, 2048], P(None, 'head'), may hold values from -0.125 to 0.125
- w_key: bfloat16 [2048, 2048], P(None, 'head'), may hold values from -0.125 to 0.125
- w_value: bfloat16 [2048, 2048], P(None, 'head'), may hold values from -0.125 to 0.125
- window: int32 [768], replicated, may hold values from 0 to 4, as said below
- global_blocks: int32 [768, 2], replicated, may hold values from 0 to 767, as said below
- file_bounds: int32 [2, 98304], replicated, may hold values from 0 to 98304, as said below
Outputs:
- attended: bfloat16 [98304, 2048], P('seq', 'head')
The draws below stay inside these ranges and needn't reach their ends.
Inputs may be any that keep to these rules, and one draw needn't show every extreme that they name: `window`: blocks fall into aligned runs of 4; in each aligned pair of runs one run has half-widths of 1 or more with one exactly 4, and the other run has all half-widths 0. `global_blocks`: every listed global block lies at most 4 blocks before or after its query block, and some lie exactly 4 away; a listed block may lie outside the query's file; in a run whose half-widths are all 0 the listed blocks lie in that run. `file_bounds`: files are runs of whole tokens holding the token itself; no file crosses a position k * 2048 - 2048 // 2, each file has at most 2048 tokens, and one file has exactly 2048.
All inputs are finite; a program needn't handle non-finite values.
Results may differ from the reference program's by a relative error of at most 0.012.
The reference program's roundings to bfloat16 on the way (of `query`, `key`, `value` and `weight`) count: a program that leaves them out, or rounds other values in their place, can miss the bound.
Values may be sent and summed in bfloat16 or wider, within the bound.
A program may use at most 128 MiB of HBM per device.

```python
import jax
import jax.numpy as jnp
from jax import lax

HEADS = 16
HEAD_DIM = 128
BLOCK = 128
GLOB = 2
BLK_DEV = 4
D = 2048
TOK_DEV = 512
TOKENS = 98304
NBLK = 768
FILE_MAX = 2048


def heavy_runs(key):
    runs = NBLK // BLK_DEV
    run_ids = jnp.arange(runs, dtype=jnp.int32)
    pair = run_ids // 2
    pick = jnp.where(pair < runs // 4, 1, 0).astype(jnp.int32)
    return run_ids % 2 == pick


def draw_tokens(key, part):
    key_c = jax.random.fold_in(jax.random.fold_in(key, 11), 2)
    values = jnp.clip(jax.random.normal(key_c, (TOKENS, D), jnp.float32), -6.0, 6.0)
    return values.astype(jnp.bfloat16)


def draw_window(key, part):
    heavy = heavy_runs(key)
    key_a, key_b = jax.random.split(jax.random.fold_in(key, 41), 2)
    block_ids = jnp.arange(NBLK, dtype=jnp.int32)
    run = block_ids // BLK_DEV
    widths = jax.random.randint(key_a, (NBLK,), 1, BLK_DEV + 1, dtype=jnp.int32)
    peak = jax.random.randint(key_b, (NBLK // BLK_DEV,), 0, BLK_DEV, dtype=jnp.int32)
    widths = jnp.where(block_ids % BLK_DEV == peak[run], BLK_DEV, widths)
    return jnp.where(heavy[run], widths, 0).astype(jnp.int32)


def draw_global_blocks(key, part):
    heavy = heavy_runs(key)
    key_a, key_b, key_c = jax.random.split(jax.random.fold_in(key, 23), 3)
    block_ids = jnp.arange(NBLK, dtype=jnp.int32)
    run = block_ids // BLK_DEV
    signs = 2 * jax.random.randint(key_a, (NBLK,), 0, 2, dtype=jnp.int32) - 1
    first = block_ids + signs * BLK_DEV
    others = block_ids[:, None] + jax.random.randint(key_b, (NBLK, GLOB - 1), -BLK_DEV, BLK_DEV + 1, dtype=jnp.int32)
    wide = jnp.clip(jnp.concatenate([first[:, None], others], axis=1), 0, NBLK - 1)
    inside = (run * BLK_DEV)[:, None] + jax.random.randint(key_c, (NBLK, GLOB), 0, BLK_DEV, dtype=jnp.int32)
    return jnp.where(heavy[run][:, None], wide, inside).astype(jnp.int32)


def draw_file_bounds(key, part):
    key_a, key_b = jax.random.split(jax.random.fold_in(key, 37), 2)
    span = FILE_MAX
    half = span // 2
    groups = TOKENS // span + 1
    cuts = jax.random.randint(key_a, (groups,), 1, span, dtype=jnp.int32)
    cuts = cuts + jnp.where(cuts % TOK_DEV == 0, 1, 0).astype(jnp.int32)
    single = jax.random.randint(key_b, (), 1, groups - 1, dtype=jnp.int32)
    cuts = jnp.where(jnp.arange(groups, dtype=jnp.int32) == single, span, cuts)
    position = jnp.arange(TOKENS, dtype=jnp.int32)
    shifted = position + half
    group = shifted // span
    offset = shifted % span
    cut_here = cuts[group]
    anchor = group * span - half
    starts = jnp.maximum(anchor + jnp.where(offset < cut_here, 0, cut_here), 0)
    ends = jnp.minimum(anchor + jnp.where(offset < cut_here, cut_here, span), TOKENS)
    return jnp.stack([starts, ends]).astype(jnp.int32)


def steps_of(rng, dims, cuts, low, high):
    def one(dim, shards_of):
        heights = jax.random.uniform(jax.random.fold_in(jax.random.fold_in(rng, 6), dim), (shards_of,), jnp.float32, low / len(cuts), high / len(cuts))
        return jnp.repeat(jnp.exp(heights), dims[dim] // shards_of).reshape((-1,) + (1,) * (len(dims) - dim - 1))

    loudness = one(*cuts[0])
    for cut in cuts[1:]:
        loudness = loudness * one(*cut)
    return loudness


def bell_draw(own_key, shape, scale, most, cuts=(), kind=jnp.bfloat16):
    values = scale * jax.random.normal(own_key, shape, jnp.float32)
    if cuts:
        values = values * steps_of(own_key, shape, cuts, -0.22, 0.18)
    return jnp.clip(values, -most, most).astype(kind)


def setup_inputs(seed: int = 0) -> dict:
    seeds = jax.random.split(jax.random.key(seed), 8)
    return {
        "tokens": draw_tokens(jax.random.fold_in(seeds[7], 71), 0),
        "w_query": bell_draw(seeds[1], (D, D), D ** -0.5, 0.125, ((1, 4),)),
        "w_key": bell_draw(seeds[2], (D, D), D ** -0.5, 0.125, ((1, 4),)),
        "w_value": bell_draw(seeds[3], (D, D), D ** -0.5, 0.125, ((1, 4),)),
        "window": draw_window(jax.random.fold_in(seeds[7], 71), 0),
        "global_blocks": draw_global_blocks(jax.random.fold_in(seeds[7], 71), 0),
        "file_bounds": draw_file_bounds(jax.random.fold_in(seeds[7], 71), 0),
    }


def reference(tokens, w_query, w_key, w_value, window, global_blocks, file_bounds):
    query = jnp.dot(tokens, w_query, preferred_element_type=jnp.float32).astype(jnp.bfloat16)
    key = jnp.dot(tokens, w_key, preferred_element_type=jnp.float32).astype(jnp.bfloat16)
    value = jnp.dot(tokens, w_value, preferred_element_type=jnp.float32).astype(jnp.bfloat16)
    query3 = query.reshape(TOKENS, HEADS, HEAD_DIM)
    margin = BLK_DEV * BLOCK
    reach = (2 * BLK_DEV + 1) * BLOCK
    key_pad = jnp.pad(key.reshape(TOKENS, HEADS, HEAD_DIM), ((margin, margin), (0, 0), (0, 0)))
    value_pad = jnp.pad(value.reshape(TOKENS, HEADS, HEAD_DIM), ((margin, margin), (0, 0), (0, 0)))
    scale = HEAD_DIM ** -0.5

    def one_block(block_id):
        first = (block_id * BLOCK).astype(jnp.int32)
        zero = jnp.zeros((), jnp.int32)
        q_rows = lax.dynamic_slice(query3, (first, zero, zero), (BLOCK, HEADS, HEAD_DIM)).astype(jnp.float32)
        k_rows = lax.dynamic_slice(key_pad, (first, zero, zero), (reach, HEADS, HEAD_DIM)).astype(jnp.float32)
        v_rows = lax.dynamic_slice(value_pad, (first, zero, zero), (reach, HEADS, HEAD_DIM)).astype(jnp.float32)
        key_pos = first - margin + jnp.arange(reach, dtype=jnp.int32)
        key_blk = jnp.floor_divide(key_pos, BLOCK)
        starts = lax.dynamic_slice(file_bounds[0], (first,), (BLOCK,))
        ends = lax.dynamic_slice(file_bounds[1], (first,), (BLOCK,))
        near = jnp.abs(block_id - key_blk) <= window[block_id]
        listed = jnp.any(global_blocks[block_id][:, None] == key_blk[None, :], axis=0)
        infile = (key_pos[None, :] >= starts[:, None]) & (key_pos[None, :] < ends[:, None])
        allowed = infile & (near | listed)[None, :]
        score = jnp.einsum("qhd,khd->hqk", q_rows, k_rows) * scale
        score = jnp.where(allowed[None], score, -jnp.inf)
        top = jnp.max(score, axis=2, keepdims=True)
        expo = jnp.exp(score - top)
        weight = (expo / jnp.sum(expo, axis=2, keepdims=True)).astype(jnp.bfloat16)
        mixed = jnp.einsum("hqk,khd->qhd", weight.astype(jnp.float32), v_rows)
        return mixed.astype(jnp.bfloat16).reshape(BLOCK, D)

    blocks = lax.map(one_block, jnp.arange(NBLK, dtype=jnp.int32))
    return blocks.reshape(TOKENS, D)
```

```python
import functools

import jax
import jax.numpy as jnp
from jax import lax
from jax.experimental import pallas as pl
from jax.experimental.pallas import tpu as pltpu
from jax.sharding import PartitionSpec as P

MESH = pl.DeviceIdType.MESH
HEAD_DIM = 128
BLOCK = 128
ROWS = 512
FEAT = 512
HALF = 256
RING = 8
HEADS = 4
SUBS = 4
SUB = HALF // SUBS
BND = 8
OTHER = 10
LONG = 5


def kernel(groups, tok, wq, wk, wv, win, glob, fb, out, big, wbuf, qbuf, kvbuf, bias, bounds,
           acc, top, total, ring_sem, side_sem, recv_sem, local_sem):
    seq = lax.axis_index("seq")
    head = lax.axis_index("head")
    group = seq // 4
    low = seq % 4
    half_id = head // 2
    core = head % 2
    y = half_id * 4 + low
    odd = low % 2
    sgn = 1 - 2 * odd

    def at(g, yy, c):
        yy = lax.rem(yy + 2 * RING, RING)
        return (g * 4 + lax.rem(yy, 4), (yy // 4) * 2 + c)

    def slot_of(yy):
        return lax.rem(yy + 2 * RING, RING)

    up, down = at(group, y + 1, core), at(group, y - 1, core)
    mate = at(group, y, 1 - core)
    side_to = at(lax.rem(group + sgn + groups, groups), y, core)
    side_from = at(lax.rem(group - sgn + groups, groups), y, core)

    own_first = pl.multiple_of(seq * ROWS, ROWS)
    loads = [
        pltpu.make_async_copy(tok, big.at[y], local_sem.at[0]),
        pltpu.make_async_copy(fb.at[:, pl.ds(own_first, ROWS)], bounds, local_sem.at[1]),
        pltpu.make_async_copy(wq, wbuf.at[:, pl.ds(0, 512)], local_sem.at[2]),
        pltpu.make_async_copy(wk, wbuf.at[:, pl.ds(512, 512)], local_sem.at[3]),
        pltpu.make_async_copy(wv, wbuf.at[:, pl.ds(1024, 512)], local_sem.at[4]),
    ]
    for load in loads:
        load.start()

    barrier = pltpu.get_barrier_semaphore()
    for peer in (up, down, mate, side_to, side_from):
        pl.semaphore_signal(barrier, inc=1, device_id=peer, device_id_type=MESH)
    pl.semaphore_wait(barrier, 5)

    waits = []

    def send(sems, count, src_slot, dst_slot, half, k, target, own=False):
        first = pl.multiple_of(half * HALF + k * SUB, SUB)
        rows = pl.ds(first, SUB)
        src = tok.at[rows] if own else big.at[src_slot, rows]
        copy = pltpu.make_async_remote_copy(
            src_ref=src,
            dst_ref=big.at[dst_slot, rows],
            send_sem=sems.at[count],
            recv_sem=recv_sem.at[dst_slot, half * SUBS + k],
            device_id=target,
            device_id_type=MESH,
        )
        copy.start()
        waits.append(copy)

    def arrived(slot, half, k):
        first = pl.multiple_of(half * HALF + k * SUB, SUB)
        ref = big.at[slot, pl.ds(first, SUB)]
        pltpu.make_async_copy(ref, ref, recv_sem.at[slot, half * SUBS + k]).wait()

    ring_n = [0]
    side_n = [0]

    def ring(src_slot, half, k, target, own=False):
        send(ring_sem, ring_n[0], src_slot, src_slot, half, k, target, own)
        ring_n[0] += 1

    def side(src_slot, dst_slot, half, k, target, own=False):
        send(side_sem, side_n[0], src_slot, dst_slot, half, k, target, own)
        side_n[0] += 1

    def to_mate(slot, half, k, own=False):
        side(slot, slot + OTHER, half, k, mate, own)

    for k in range(SUBS):
        ring(y, 0, k, up, True)
        ring(y, 1, k, down, True)
    for k in range(SUBS):
        ring(y, 1, k, up, True)
        ring(y, 0, k, down, True)
    for half in range(2):
        for k in range(SUBS):
            to_mate(y, half, k, True)

    def pick(if_even, if_odd):
        return jnp.where(odd == 1, if_odd, if_even)

    def route(slot, half, k, cross, dst):
        side(
            slot,
            jnp.where(cross == 1, dst, slot + OTHER),
            half,
            k,
            tuple(jnp.where(cross == 1, a, b) for a, b in zip(side_to, mate)),
        )

    def step(s):
        plus, minus = slot_of(y - s), slot_of(y + s)
        for k in range(SUBS):
            arrived(plus, 0, k)
            if s < LONG:
                ring(plus, 0, k, up)
            arrived(minus, 1, k)
            if s < LONG:
                ring(minus, 1, k, down)
            if s == 1:
                route(plus, 0, k, 1 - odd, BND)
                route(minus, 1, k, odd, BND)
            elif s == 3:
                route(plus, 0, k, odd, BND + 1)
                route(minus, 1, k, 1 - odd, BND + 1)
            elif s == 4:
                to_mate(plus, 0, k)
                to_mate(minus, 1, k)
            elif s == 5:
                route(plus, 0, k, 1 - odd, BND + 1)
                route(minus, 1, k, odd, BND + 1)
        if s == 1:
            for k in range(SUBS):
                arrived(plus, 1, k)
                route(plus, 1, k, 1 - odd, BND)
                arrived(minus, 0, k)
                route(minus, 0, k, odd, BND)

    def bnd_arrived(which, half):
        for k in range(SUBS):
            arrived(BND + which, half, k)
            to_mate(BND + which, half, k)

    def mate_arrived(slot, half):
        for k in range(SUBS):
            arrived(slot + OTHER, half, k)

    g_near = half_id * 2
    g_far = (1 - half_id) * 2

    def project(near, far, half, run, with_query):
        rows = pl.ds(pl.multiple_of(half * HALF, HALF), HALF)
        parts = [(near, g_near + core), (near + OTHER, g_near + 1 - core), (far, g_far + core), (far + OTHER, g_far + 1 - core)]

        def tile(c):
            res = None
            for slot, g in parts:
                w = wbuf[pl.ds(pl.multiple_of(g * FEAT, FEAT), FEAT), c * 512:(c + 1) * 512]
                part = jnp.dot(big[slot, rows, :], w, preferred_element_type=jnp.float32)
                res = part if res is None else res + part
            return res.astype(jnp.bfloat16)

        if with_query:
            qbuf[rows, :] = tile(0)
        dst = pl.ds(pl.multiple_of(run * ROWS + half * HALF, HALF), HALF)
        kvbuf[dst, 0:512] = tile(1)
        kvbuf[dst, 512:1024] = tile(2)

    def make_bias():
        lane = lax.broadcasted_iota(jnp.int32, (BLOCK, BLOCK), 1)
        for p in range(4):
            cols = slice(p * BLOCK, (p + 1) * BLOCK)
            start = jnp.broadcast_to(bounds[0:1, cols].astype(jnp.float32), (BLOCK, BLOCK)).T.astype(jnp.int32)
            end = jnp.broadcast_to(bounds[1:2, cols].astype(jnp.float32), (BLOCK, BLOCK)).T.astype(jnp.int32)
            me = seq * 4 + p
            width, g0, g1 = win[me], glob[0, me], glob[1, me]
            for e in range(12):
                blk = seq * 4 - 4 + e
                ok = (abs(e - 4 - p) <= width) | (g0 == blk) | (g1 == blk)
                pos = jnp.where(ok, blk * BLOCK, -(1 << 20)) + lane
                keep = (pos >= start) & (pos < end)
                bias[cols, e * BLOCK:(e + 1) * BLOCK] = jnp.where(keep, 0.0, -jnp.inf)

    def attend(run, first_key, keys, is_first):
        k_rows = pl.ds(pl.multiple_of(run * ROWS + first_key, HALF), keys)

        def body(p, carry):
            q_rows = pl.ds(pl.multiple_of(p * BLOCK, BLOCK), BLOCK)
            mask = bias[q_rows, pl.ds(pl.multiple_of(run * ROWS + first_key, HALF), keys)]
            for h in range(HEADS):
                hc = slice(h * HEAD_DIM, (h + 1) * HEAD_DIM)
                key = kvbuf[k_rows, hc]
                value = kvbuf[k_rows, 512 + h * HEAD_DIM:512 + (h + 1) * HEAD_DIM]
                score = lax.dot_general(
                    qbuf[q_rows, hc], key, (((1,), (1,)), ((), ())), preferred_element_type=jnp.float32
                ) * HEAD_DIM ** -0.5 + mask
                high = jnp.broadcast_to(jnp.max(score, axis=1, keepdims=True), (BLOCK, HEAD_DIM))
                if not is_first:
                    old = top[h, q_rows, :]
                    high = jnp.maximum(high, old)
                expo = jnp.exp(score - high[:, 0:1])
                sums = jnp.broadcast_to(jnp.sum(expo, axis=1, keepdims=True), (BLOCK, HEAD_DIM))
                mixed = jnp.dot(expo.astype(jnp.bfloat16), value, preferred_element_type=jnp.float32)
                if not is_first:
                    keep = jnp.exp(old - high)
                    sums = sums + keep * total[h, q_rows, :]
                    mixed = mixed + keep * acc[h, q_rows, :]
                top[h, q_rows, :] = high
                total[h, q_rows, :] = sums
                acc[h, q_rows, :] = mixed
            return carry

        lax.fori_loop(0, 4, body, 0)

    even = 1 - odd
    h_f, h_b = odd, 1 - odd
    own_far = slot_of(y + 4)
    pair_near, pair_far = slot_of(y + sgn), slot_of(y - 3 * sgn)
    pair_run, bnd_run = 1 + sgn, 1 - sgn

    loads[1].wait()
    make_bias()
    step(1)
    for load in loads[2:] + loads[:1]:
        load.wait()
    step(2)
    bnd_arrived(0, h_f)
    bnd_arrived(0, h_b)
    step(3)
    for half in range(2):
        mate_arrived(y, half)
    mate_arrived(pair_near, h_f)
    mate_arrived(pair_far, h_f)
    project(pair_near, pair_far, h_f, pair_run, False)
    step(4)
    bnd_arrived(1, h_b)
    for half in range(2):
        mate_arrived(own_far, half)
        project(y, own_far, half, 1, True)
    attend(1, 0, ROWS, True)
    attend(pair_run, h_f * HALF, HALF, False)
    step(5)
    for half in (h_f, h_b):
        mate_arrived(BND, half)
    mate_arrived(BND + 1, h_b)
    project(BND + 1, BND, h_b, bnd_run, False)
    attend(bnd_run, h_b * HALF, HALF, False)
    mate_arrived(pair_near, h_b)
    mate_arrived(pair_far, h_b)
    project(pair_near, pair_far, h_b, pair_run, False)
    attend(pair_run, h_b * HALF, HALF, False)
    bnd_arrived(1, h_f)
    mate_arrived(BND + 1, h_f)
    project(BND + 1, BND, h_f, bnd_run, False)
    attend(bnd_run, h_f * HALF, HALF, False)
    for h in range(HEADS):
        out[:, h * HEAD_DIM:(h + 1) * HEAD_DIM] = (acc[h] / total[h]).astype(jnp.bfloat16)
    for copy in waits:
        copy.wait_send()


def local(groups, tokens, w_query, w_key, w_value, window, global_blocks, file_bounds):
    anywhere = pl.BlockSpec(memory_space=pl.ANY)
    scalars = pl.BlockSpec(memory_space=pltpu.SMEM)
    return pl.pallas_call(
        functools.partial(kernel, groups),
        out_shape=jax.ShapeDtypeStruct((ROWS, FEAT), jnp.bfloat16),
        in_specs=[anywhere] * 4 + [scalars] * 2 + [anywhere],
        out_specs=pl.BlockSpec(memory_space=pltpu.VMEM),
        scratch_shapes=[
            pltpu.VMEM((20, ROWS, FEAT), jnp.bfloat16),
            pltpu.VMEM((2048, 1536), jnp.bfloat16),
            pltpu.VMEM((ROWS, FEAT), jnp.bfloat16),
            pltpu.VMEM((3 * ROWS, 2 * FEAT), jnp.bfloat16),
            pltpu.VMEM((ROWS, 3 * ROWS), jnp.float32),
            pltpu.VMEM((2, ROWS), jnp.int32),
            pltpu.VMEM((HEADS, ROWS, HEAD_DIM), jnp.float32),
            pltpu.VMEM((HEADS, ROWS, HEAD_DIM), jnp.float32),
            pltpu.VMEM((HEADS, ROWS, HEAD_DIM), jnp.float32),
            pltpu.SemaphoreType.DMA((12 * SUBS,)),
            pltpu.SemaphoreType.DMA((16 * SUBS,)),
            pltpu.SemaphoreType.DMA((20, 2 * SUBS)),
            pltpu.SemaphoreType.DMA((5,)),
        ],
        compiler_params=pltpu.CompilerParams(
            collective_id=0, has_side_effects=True, vmem_limit_bytes=56 << 20
        ),
        cost_estimate=pl.CostEstimate(flops=9_000_000_000, bytes_accessed=8_000_000, transcendentals=3_000_000),
        name="gather_project_attend",
    )(tokens, w_query, w_key, w_value, window, global_blocks.T, file_bounds)


def solution(mesh):
    placed = (P("seq", "head"), P(None, "head"), P(None, "head"), P(None, "head"), P(), P(), P())
    return jax.shard_map(
        functools.partial(local, mesh.shape["seq"] // 4),
        mesh=mesh, in_specs=placed, out_specs=P("seq", "head"), check_vma=False,
    )
```

```python
import functools

import jax
import jax.numpy as jnp
from jax import lax
from jax.experimental import pallas as pl
from jax.experimental.pallas import tpu as pltpu
from jax.sharding import PartitionSpec as P

MESH = pl.DeviceIdType.MESH
HEAD_DIM = 128
BLOCK = 128
ROWS = 512
FEAT = 512
HALF = 256
RING = 8
HEADS = 4
SUBS = 4
SUB = HALF // SUBS
BND = 8
OTHER = 10
LONG = 5
SCALE = HEAD_DIM ** -0.5 * 1.4426950408889634
LOW = -1e30


def kernel(groups, tok, wq, wk, wv, win, glob, fb, out, big, wbuf, qbuf, kbuf, vbuf, bias, bounds,
           part_own, part_pair, part_bnd, acc, top, ring_sem, side_sem, recv_sem, local_sem):
    seq = lax.axis_index("seq")
    head = lax.axis_index("head")
    group = seq // 4
    low = seq % 4
    half_id = head // 2
    core = head % 2
    y = half_id * 4 + low
    odd = low % 2
    sgn = 1 - 2 * odd
    h_f, h_b = odd, 1 - odd

    def slot_of(yy):
        return lax.rem(yy + 2 * RING, RING)

    def at(g, yy, c):
        yy = slot_of(yy)
        return (g * 4 + lax.rem(yy, 4), (yy // 4) * 2 + c)

    ahead, behind = at(group, y + sgn, core), at(group, y - sgn, core)
    mate = at(group, y, 1 - core)
    next_group = lax.rem(group + sgn + groups, groups)
    last_group = lax.rem(group - sgn + groups, groups)
    side, side_mate = at(next_group, y, core), at(next_group, y, 1 - core)

    own_first = pl.multiple_of(seq * ROWS, ROWS)
    load_tok = pltpu.make_async_copy(tok, big.at[y], local_sem.at[0])
    load_fb = pltpu.make_async_copy(fb.at[:, pl.ds(own_first, ROWS)], bounds, local_sem.at[1])
    load_w = [
        pltpu.make_async_copy(w, wbuf.at[:, pl.ds(i * FEAT, FEAT)], local_sem.at[2 + i])
        for i, w in enumerate((wq, wk, wv))
    ]

    barrier = pltpu.get_barrier_semaphore()
    peers = (ahead, behind, mate, side, side_mate, at(last_group, y, core), at(last_group, y, 1 - core))
    for peer in peers:
        pl.semaphore_signal(barrier, inc=1, device_id=peer, device_id_type=MESH)
    load_tok.start()
    load_fb.start()
    pl.semaphore_wait(barrier, len(peers))

    waits = []
    counts = {"ring": 0, "side": 0}

    def send(kind, src_slot, dst_slot, half, k, target, own=False):
        rows = pl.ds(pl.multiple_of(half * HALF + k * SUB, SUB), SUB)
        copy = pltpu.make_async_remote_copy(
            src_ref=tok.at[rows] if own else big.at[src_slot, rows],
            dst_ref=big.at[dst_slot, rows],
            send_sem=(ring_sem if kind == "ring" else side_sem).at[counts[kind]],
            recv_sem=recv_sem.at[dst_slot, half * SUBS + k],
            device_id=target,
            device_id_type=MESH,
        )
        copy.start()
        counts[kind] += 1
        waits.append(copy)

    def to_mate(slot, half, k, own=False):
        send("side", slot, slot + OTHER, half, k, mate, own)

    def arrived(slot, half, k):
        ref = big.at[slot, pl.ds(pl.multiple_of(half * HALF + k * SUB, SUB), SUB)]
        pltpu.make_async_copy(ref, ref, recv_sem.at[slot, half * SUBS + k]).wait()

    def mate_arrived(slot, half):
        for k in range(SUBS):
            arrived(slot + OTHER, half, k)

    def bnd_arrived(which, half):
        for k in range(SUBS):
            arrived(BND + which, half, k)
            to_mate(BND + which, half, k)

    def step(s, pieces=range(SUBS)):
        f, b = slot_of(y - s * sgn), slot_of(y + s * sgn)
        for k in pieces:
            arrived(f, h_f, k)
            if s < LONG:
                send("ring", f, f, h_f, k, ahead)
            if s == 1:
                send("side", f, BND, h_f, k, side)
            elif s in (3, 4):
                to_mate(f, h_f, k)
            elif s == 5:
                send("side", f, BND + 1, h_f, k, side)
                send("side", f, BND + 1 + OTHER, h_f, k, side_mate)
            arrived(b, h_b, k)
            if s < LONG:
                send("ring", b, b, h_b, k, behind)
            if s == 3:
                send("side", b, BND + 1, h_b, k, side)
            elif s != 2:
                to_mate(b, h_b, k)
        if s == 1:
            for k in pieces:
                arrived(f, h_b, k)
                send("side", f, BND, h_b, k, side)
                arrived(b, h_f, k)
                to_mate(b, h_f, k)

    g_near = half_id * 2
    g_far = 2 - g_near

    def rows_of(half):
        return pl.ds(pl.multiple_of(half * HALF, HALF), HALF)

    def product(slot, g, half, tile):
        def one(s, gg):
            w = wbuf[pl.ds(pl.multiple_of(gg * FEAT, FEAT), FEAT), tile * FEAT:(tile + 1) * FEAT]
            return jnp.dot(big[s, rows_of(half), :], w, preferred_element_type=jnp.float32)

        return one(slot, g + core) + one(slot + OTHER, g + 1 - core)

    def first_part(part, slot, g, half, tiles):
        for i, tile in enumerate(tiles):
            part[rows_of(half), i * FEAT:(i + 1) * FEAT] = product(slot, g, half, tile)

    def second_part(part, slot, g, half, tiles, run):
        keys = pl.ds(pl.multiple_of(run * ROWS + half * HALF, HALF), HALF)
        for i, tile in enumerate(tiles):
            whole = part[rows_of(half), i * FEAT:(i + 1) * FEAT] + product(slot, g, half, tile)
            if tile == 0:
                qbuf[rows_of(half), :] = whole.astype(jnp.bfloat16)
            elif tile == 1:
                kbuf[keys, :] = whole.astype(jnp.bfloat16)
            else:
                for h in range(HEADS):
                    vbuf[h, 0:HEAD_DIM, keys] = whole[:, h * HEAD_DIM:(h + 1) * HEAD_DIM].T.astype(jnp.bfloat16)

    def make_bias():
        for e in range(12):
            blk = seq * 4 - 4 + e
            row = lax.broadcasted_iota(jnp.int32, (BLOCK, BLOCK), 0)
            for p in range(4):
                cols = slice(p * BLOCK, (p + 1) * BLOCK)
                me = seq * 4 + p
                ok = (abs(e - 4 - p) <= win[me]) | (glob[0, me] == blk) | (glob[1, me] == blk)
                pos = jnp.where(ok, blk * BLOCK, -(1 << 20)) + row
                keep = (pos >= bounds[0:1, cols]) & (pos < bounds[1:2, cols])
                bias[e * BLOCK:(e + 1) * BLOCK, cols] = jnp.where(keep, 0.0, -jnp.inf)

    def attend(run, first_key, keys, query_half=None, heads=range(HEADS)):
        k_rows = pl.ds(pl.multiple_of(run * ROWS + first_key, HALF), keys)
        q_rows = slice(None) if query_half is None else rows_of(query_half)
        mask = bias[k_rows, q_rows]
        for h in heads:
            hc = slice(h * HEAD_DIM, (h + 1) * HEAD_DIM)
            score = lax.dot_general(
                kbuf[k_rows, hc], qbuf[q_rows, hc], (((1,), (1,)), ((), ())), preferred_element_type=jnp.float32
            ) + mask
            old = top[h, :, q_rows]
            high = jnp.maximum(jnp.max(score, axis=0, keepdims=True), old)
            expo = jnp.exp2((score - high) * SCALE).astype(jnp.bfloat16)
            mixed = jnp.dot(vbuf[h, :, k_rows], expo, preferred_element_type=jnp.float32)
            acc[h, :, q_rows] = mixed + jnp.exp2((old - high) * SCALE) * acc[h, :, q_rows]
            top[h, :, q_rows] = high

    def finish(half):
        for h in range(HEADS):
            mean = acc[h, 0:HEAD_DIM, rows_of(half)] / acc[h, HEAD_DIM:HEAD_DIM + 1, rows_of(half)]
            out[rows_of(half), h * HEAD_DIM:(h + 1) * HEAD_DIM] = mean.T.astype(jnp.bfloat16)

    own_far = slot_of(y + 4)
    pair_near, pair_far = slot_of(y + sgn), slot_of(y - 3 * sgn)
    pair_run, bnd_run = 1 + sgn, 1 - sgn
    both, keyval = (0, 1), (1, 2)

    for k in range(SUBS):
        send("ring", y, y, h_f, k, ahead, True)
        send("ring", y, y, h_b, k, behind, True)
    for k in range(SUBS):
        send("ring", y, y, h_b, k, ahead, True)
        send("ring", y, y, h_f, k, behind, True)
    for half in both:
        for k in range(SUBS):
            to_mate(y, half, k, True)
    for load in load_w:
        load.start()
    acc[...] = jnp.zeros_like(acc)
    top[...] = jnp.full_like(top, LOW)
    vbuf[:, HEAD_DIM:, :] = jnp.ones_like(vbuf[:, HEAD_DIM:, :])
    load_fb.wait()
    make_bias()
    for load in load_w:
        load.wait()
    load_tok.wait()
    for half in both:
        mate_arrived(y, half)
        first_part(part_own, y, g_near, half, (0, 1, 2))
    step(1)
    for half in both:
        mate_arrived(pair_near, half)
        first_part(part_pair, pair_near, g_near, half, keyval)
    step(2)
    for half in (h_f, h_b):
        bnd_arrived(0, half)
    step(3)
    for half in (h_f, h_b):
        mate_arrived(BND, half)
        first_part(part_bnd, BND, g_far, half, keyval)
    mate_arrived(pair_far, h_f)
    second_part(part_pair, pair_far, g_far, h_f, keyval, pair_run)
    step(4)
    bnd_arrived(1, h_b)
    for half in both:
        mate_arrived(own_far, half)
        second_part(part_own, own_far, g_far, half, (0, 1, 2), 1)
    step(5, (0,))
    attend(1, 0, ROWS, None, (0, 1))
    step(5, (1,))
    attend(1, 0, ROWS, None, (2, 3))
    step(5, (2,))
    mate_arrived(BND + 1, h_b)
    second_part(part_bnd, BND + 1, g_near, h_b, keyval, bnd_run)
    step(5, (3,))
    attend(pair_run, h_f * HALF, HALF)
    attend(bnd_run, h_b * HALF, HALF)
    mate_arrived(pair_far, h_b)
    second_part(part_pair, pair_far, g_far, h_b, keyval, pair_run)
    attend(pair_run, h_b * HALF, HALF, h_b)
    finish(h_b)
    for k in range(SUBS):
        arrived(BND + 1, h_f, k)
    mate_arrived(BND + 1, h_f)
    second_part(part_bnd, BND + 1, g_near, h_f, keyval, bnd_run)
    attend(bnd_run, h_f * HALF, HALF, h_f)
    finish(h_f)
    for copy in waits:
        copy.wait_send()


def local(groups, tokens, w_query, w_key, w_value, window, global_blocks, file_bounds):
    anywhere = pl.BlockSpec(memory_space=pl.ANY)
    scalars = pl.BlockSpec(memory_space=pltpu.SMEM)
    return pl.pallas_call(
        functools.partial(kernel, groups),
        out_shape=jax.ShapeDtypeStruct((ROWS, FEAT), jnp.bfloat16),
        in_specs=[anywhere] * 4 + [scalars] * 2 + [anywhere],
        out_specs=pl.BlockSpec(memory_space=pltpu.VMEM),
        scratch_shapes=[
            pltpu.VMEM((20, ROWS, FEAT), jnp.bfloat16),
            pltpu.VMEM((2048, 3 * FEAT), jnp.bfloat16),
            pltpu.VMEM((ROWS, FEAT), jnp.bfloat16),
            pltpu.VMEM((3 * ROWS, FEAT), jnp.bfloat16),
            pltpu.VMEM((HEADS, HEAD_DIM + 16, 3 * ROWS), jnp.bfloat16),
            pltpu.VMEM((3 * ROWS, ROWS), jnp.float32),
            pltpu.VMEM((2, ROWS), jnp.int32),
            pltpu.VMEM((ROWS, 3 * FEAT), jnp.float32),
            pltpu.VMEM((ROWS, 2 * FEAT), jnp.float32),
            pltpu.VMEM((ROWS, 2 * FEAT), jnp.float32),
            pltpu.VMEM((HEADS, HEAD_DIM + 16, ROWS), jnp.float32),
            pltpu.VMEM((HEADS, 1, ROWS), jnp.float32),
            pltpu.SemaphoreType.DMA((12 * SUBS,)),
            pltpu.SemaphoreType.DMA((16 * SUBS,)),
            pltpu.SemaphoreType.DMA((20, 2 * SUBS)),
            pltpu.SemaphoreType.DMA((5,)),
        ],
        compiler_params=pltpu.CompilerParams(
            collective_id=0, has_side_effects=True, vmem_limit_bytes=56 << 20
        ),
        cost_estimate=pl.CostEstimate(flops=9_000_000_000, bytes_accessed=8_000_000, transcendentals=3_000_000),
        name="gather_project_attend",
    )(tokens, w_query, w_key, w_value, window, global_blocks.T, file_bounds)


def solution(mesh):
    placed = (P("seq", "head"), P(None, "head"), P(None, "head"), P(None, "head"), P(), P(), P())
    return jax.shard_map(
        functools.partial(local, mesh.shape["seq"] // 4),
        mesh=mesh, in_specs=placed, out_specs=P("seq", "head"), check_vma=False,
    )
```

```python
import functools

import jax
import jax.numpy as jnp
from jax import lax
from jax.experimental import pallas as pl
from jax.experimental.pallas import tpu as pltpu
from jax.sharding import PartitionSpec as P

MESH = pl.DeviceIdType.MESH
HEAD_DIM = 128
BLOCK = 128
ROWS = 512
FEAT = 512
HALF = 256
RING = 8
HEADS = 4
SUBS = 4
SUB = HALF // SUBS
BND = 8
OTHER = 10
LONG = 5
SCALE = HEAD_DIM ** -0.5 * 1.4426950408889634
LOW = -1e30


def kernel(groups, tok, wq, wk, wv, win, glob, fb, out, big, wbuf, qbuf, kbuf, vbuf, bias, bounds,
           part_own, part_pair, part_bnd, acc, top, ring_sem, side_sem, recv_sem, local_sem):
    seq = lax.axis_index("seq")
    head = lax.axis_index("head")
    group = seq // 4
    low = seq % 4
    half_id = head // 2
    core = head % 2
    y = half_id * 4 + low
    odd = low % 2
    sgn = 1 - 2 * odd
    h_f, h_b = odd, 1 - odd

    def slot_of(yy):
        return lax.rem(yy + 2 * RING, RING)

    def at(g, yy, c):
        yy = slot_of(yy)
        return (g * 4 + lax.rem(yy, 4), (yy // 4) * 2 + c)

    ahead, behind = at(group, y + sgn, core), at(group, y - sgn, core)
    mate = at(group, y, 1 - core)
    next_group = lax.rem(group + sgn + groups, groups)
    last_group = lax.rem(group - sgn + groups, groups)
    side = at(next_group, y, core)

    own_first = pl.multiple_of(seq * ROWS, ROWS)
    load_tok = pltpu.make_async_copy(tok, big.at[y], local_sem.at[0])
    load_fb = pltpu.make_async_copy(fb.at[:, pl.ds(own_first, ROWS)], bounds, local_sem.at[1])
    load_w = [
        pltpu.make_async_copy(w, wbuf.at[:, pl.ds(i * FEAT, FEAT)], local_sem.at[2 + i])
        for i, w in enumerate((wq, wk, wv))
    ]

    barrier = pltpu.get_barrier_semaphore()
    peers = (ahead, behind, mate, side, at(last_group, y, core))
    for peer in peers:
        pl.semaphore_signal(barrier, inc=1, device_id=peer, device_id_type=MESH)
    load_tok.start()
    load_fb.start()
    pl.semaphore_wait(barrier, len(peers))

    waits = []
    counts = {"ring": 0, "side": 0}

    def rows_of(half, k=None):
        if k is None:
            return pl.ds(pl.multiple_of(half * HALF, HALF), HALF)
        return pl.ds(pl.multiple_of(half * HALF + k * SUB, SUB), SUB)

    def send(kind, src_slot, dst_slot, half, k, target, own=False):
        rows = rows_of(half, k)
        copy = pltpu.make_async_remote_copy(
            src_ref=tok.at[rows] if own else big.at[src_slot, rows],
            dst_ref=big.at[dst_slot, rows],
            send_sem=(ring_sem if kind == "ring" else side_sem).at[counts[kind]],
            recv_sem=recv_sem.at[dst_slot, half * SUBS + (k or 0)],
            device_id=target,
            device_id_type=MESH,
        )
        copy.start()
        counts[kind] += 1
        waits.append(copy)

    def to_mate(slot, half, own=False, k=None):
        send("side", slot, slot + OTHER, half, k, mate, own)

    def arrived(slot, half, k=None):
        ref = big.at[slot, rows_of(half, k)]
        pltpu.make_async_copy(ref, ref, recv_sem.at[slot, half * SUBS + (k or 0)]).wait()

    def mate_arrived(slot, half):
        arrived(slot + OTHER, half)

    def step(s, pieces=range(SUBS)):
        f, b = slot_of(y - s * sgn), slot_of(y + s * sgn)
        for k in pieces:
            arrived(f, h_f, k)
            if s < LONG:
                send("ring", f, f, h_f, k, ahead)
            else:
                send("side", f, BND + 1, h_f, k, side)
            arrived(b, h_b, k)
            if s < LONG:
                send("ring", b, b, h_b, k, behind)
        if SUBS - 1 not in pieces:
            return
        if s == 1:
            send("side", f, BND, h_f, None, side)
        elif s in (3, 4):
            to_mate(f, h_f)
        if s == 3:
            send("side", b, BND + 1, h_b, None, side)
        elif s != 2:
            to_mate(b, h_b)
    def short_way():
        f, b = slot_of(y - sgn), slot_of(y + sgn)
        arrived(f, h_b)
        send("side", f, BND, h_b, None, side)
        arrived(b, h_f)
        to_mate(b, h_f)

    def bnd_arrived(k):
        arrived(BND + 1, h_f, k)
        to_mate(BND + 1, h_f, False, k)

    g_near = half_id * 2
    g_far = 2 - g_near

    def product(slot, g, half, tile):
        def one(s, gg):
            w = wbuf[pl.ds(pl.multiple_of(gg * FEAT, FEAT), FEAT), tile * FEAT:(tile + 1) * FEAT]
            return jnp.dot(big[s, rows_of(half), :], w, preferred_element_type=jnp.float32)

        return one(slot, g + core) + one(slot + OTHER, g + 1 - core)

    def first_part(part, slot, g, half, tiles):
        for i, tile in enumerate(tiles):
            part[rows_of(half), i * FEAT:(i + 1) * FEAT] = product(slot, g, half, tile)

    def second_part(part, slot, g, half, tiles, run):
        keys = pl.ds(pl.multiple_of(run * ROWS + half * HALF, HALF), HALF)
        for i, tile in enumerate(tiles):
            whole = part[rows_of(half), i * FEAT:(i + 1) * FEAT] + product(slot, g, half, tile)
            if tile == 0:
                qbuf[rows_of(half), :] = whole.astype(jnp.bfloat16)
            elif tile == 1:
                kbuf[keys, :] = whole.astype(jnp.bfloat16)
            else:
                for h in range(HEADS):
                    vbuf[h, 0:HEAD_DIM, keys] = whole[:, h * HEAD_DIM:(h + 1) * HEAD_DIM].T.astype(jnp.bfloat16)

    def make_bias():
        for e in range(12):
            blk = seq * 4 - 4 + e
            row = lax.broadcasted_iota(jnp.int32, (BLOCK, BLOCK), 0)
            for p in range(4):
                cols = slice(p * BLOCK, (p + 1) * BLOCK)
                me = seq * 4 + p
                ok = (abs(e - 4 - p) <= win[me]) | (glob[0, me] == blk) | (glob[1, me] == blk)
                pos = jnp.where(ok, blk * BLOCK, -(1 << 20)) + row
                keep = (pos >= bounds[0:1, cols]) & (pos < bounds[1:2, cols])
                bias[e * BLOCK:(e + 1) * BLOCK, cols] = jnp.where(keep, 0.0, -jnp.inf)

    def attend(run, first_key, keys, query_half=None, heads=range(HEADS)):
        k_rows = pl.ds(pl.multiple_of(run * ROWS + first_key, HALF), keys)
        q_rows = slice(None) if query_half is None else rows_of(query_half)
        mask = bias[k_rows, q_rows]
        for h in heads:
            hc = slice(h * HEAD_DIM, (h + 1) * HEAD_DIM)
            score = lax.dot_general(
                kbuf[k_rows, hc], qbuf[q_rows, hc], (((1,), (1,)), ((), ())), preferred_element_type=jnp.float32
            ) + mask
            old = top[h, :, q_rows]
            high = jnp.maximum(jnp.max(score, axis=0, keepdims=True), old)
            expo = jnp.exp2((score - high) * SCALE).astype(jnp.bfloat16)
            mixed = jnp.dot(vbuf[h, :, k_rows], expo, preferred_element_type=jnp.float32)
            acc[h, :, q_rows] = mixed + jnp.exp2((old - high) * SCALE) * acc[h, :, q_rows]
            top[h, :, q_rows] = high

    def finish(half):
        for h in range(HEADS):
            mean = acc[h, 0:HEAD_DIM, rows_of(half)] / acc[h, HEAD_DIM:HEAD_DIM + 1, rows_of(half)]
            out[rows_of(half), h * HEAD_DIM:(h + 1) * HEAD_DIM] = mean.T.astype(jnp.bfloat16)

    own_far = slot_of(y + 4)
    pair_near, pair_far = slot_of(y + sgn), slot_of(y - 3 * sgn)
    pair_run, bnd_run = 1 + sgn, 1 - sgn
    both, keyval = (0, 1), (1, 2)

    for k in range(SUBS):
        send("ring", y, y, h_f, k, ahead, True)
        send("ring", y, y, h_b, k, behind, True)
    for half in both:
        to_mate(y, half, True)
    for load in load_w:
        load.start()
    acc[...] = jnp.zeros_like(acc)
    top[...] = jnp.full_like(top, LOW)
    vbuf[:, HEAD_DIM:, :] = jnp.ones_like(vbuf[:, HEAD_DIM:, :])
    load_fb.wait()
    make_bias()
    load_tok.wait()
    step(1)
    for load in load_w:
        load.wait()
    mate_arrived(y, 0)
    first_part(part_own, y, g_near, 0, (0, 1, 2))
    step(2)
    arrived(BND, h_f)
    to_mate(BND, h_f)
    mate_arrived(y, 1)
    first_part(part_own, y, g_near, 1, (0, 1, 2))
    mate_arrived(pair_near, h_b)
    first_part(part_pair, pair_near, g_near, h_b, keyval)
    step(3)
    send("ring", y, y, h_b, None, ahead, True)
    send("ring", y, y, h_f, None, behind, True)
    mate_arrived(BND, h_f)
    first_part(part_bnd, BND, g_far, h_f, keyval)
    mate_arrived(pair_far, h_f)
    first_part(part_pair, pair_far, g_far, h_f, keyval)
    step(4)
    arrived(BND + 1, h_b)
    to_mate(BND + 1, h_b)
    for half in both:
        mate_arrived(own_far, half)
        second_part(part_own, own_far, g_far, half, (0, 1, 2), 1)
    attend(1, 0, ROWS, None, (0, 1))
    short_way()
    attend(1, 0, ROWS, None, (2, 3))
    step(5, (0,))
    mate_arrived(BND + 1, h_b)
    first_part(part_bnd, BND + 1, g_near, h_b, keyval)
    step(5, (1,))
    mate_arrived(pair_near, h_f)
    second_part(part_pair, pair_near, g_near, h_f, keyval, pair_run)
    step(5, (2,))
    arrived(BND, h_b)
    to_mate(BND, h_b)
    attend(pair_run, h_f * HALF, HALF)
    step(5, (3,))
    mate_arrived(BND, h_b)
    second_part(part_bnd, BND, g_far, h_b, keyval, bnd_run)
    bnd_arrived(0)
    bnd_arrived(1)
    attend(bnd_run, h_b * HALF, HALF)
    bnd_arrived(2)
    mate_arrived(pair_far, h_b)
    second_part(part_pair, pair_far, g_far, h_b, keyval, pair_run)
    bnd_arrived(3)
    attend(pair_run, h_b * HALF, HALF, h_b)
    finish(h_b)
    for k in range(SUBS):
        arrived(BND + 1 + OTHER, h_f, k)
    second_part(part_bnd, BND + 1, g_near, h_f, keyval, bnd_run)
    attend(bnd_run, h_f * HALF, HALF, h_f)
    finish(h_f)
    for copy in waits:
        copy.wait_send()


def local(groups, tokens, w_query, w_key, w_value, window, global_blocks, file_bounds):
    anywhere = pl.BlockSpec(memory_space=pl.ANY)
    scalars = pl.BlockSpec(memory_space=pltpu.SMEM)
    return pl.pallas_call(
        functools.partial(kernel, groups),
        out_shape=pltpu.VMEM((ROWS, FEAT), jnp.bfloat16),
        in_specs=[anywhere] * 4 + [scalars] * 2 + [anywhere],
        out_specs=pl.BlockSpec(memory_space=pltpu.VMEM),
        scratch_shapes=[
            pltpu.VMEM((20, ROWS, FEAT), jnp.bfloat16),
            pltpu.VMEM((2048, 3 * FEAT), jnp.bfloat16),
            pltpu.VMEM((ROWS, FEAT), jnp.bfloat16),
            pltpu.VMEM((3 * ROWS, FEAT), jnp.bfloat16),
            pltpu.VMEM((HEADS, HEAD_DIM + 16, 3 * ROWS), jnp.bfloat16),
            pltpu.VMEM((3 * ROWS, ROWS), jnp.float32),
            pltpu.VMEM((2, ROWS), jnp.int32),
            pltpu.VMEM((ROWS, 3 * FEAT), jnp.float32),
            pltpu.VMEM((ROWS, 2 * FEAT), jnp.float32),
            pltpu.VMEM((ROWS, 2 * FEAT), jnp.float32),
            pltpu.VMEM((HEADS, HEAD_DIM + 16, ROWS), jnp.float32),
            pltpu.VMEM((HEADS, 1, ROWS), jnp.float32),
            pltpu.SemaphoreType.DMA((10 * SUBS + 2,)),
            pltpu.SemaphoreType.DMA((14 + 2 * SUBS,)),
            pltpu.SemaphoreType.DMA((20, 2 * SUBS)),
            pltpu.SemaphoreType.DMA((5,)),
        ],
        compiler_params=pltpu.CompilerParams(
            collective_id=0, has_side_effects=True, vmem_limit_bytes=56 << 20
        ),
        cost_estimate=pl.CostEstimate(flops=9_000_000_000, bytes_accessed=8_000_000, transcendentals=3_000_000),
        name="gather_project_attend",
    )(tokens, w_query, w_key, w_value, window, global_blocks.T, file_bounds)


def solution(mesh):
    placed = (P("seq", "head"), P(None, "head"), P(None, "head"), P(None, "head"), P(), P(), P())
    return jax.shard_map(
        functools.partial(local, mesh.shape["seq"] // 4),
        mesh=mesh, in_specs=placed, out_specs=P("seq", "head"), check_vma=False,
    )
```

```python
import functools

import jax
import jax.numpy as jnp
from jax import lax
from jax.experimental import pallas as pl
from jax.experimental.pallas import tpu as pltpu
from jax.sharding import PartitionSpec as P

MESH = pl.DeviceIdType.MESH
HEAD_DIM = 128
BLOCK = 128
ROWS = 512
FEAT = 512
HALF = 256
RING = 8
HEADS = 4
SUBS = 4
SUB = HALF // SUBS
BND = 8
OTHER = 10
LONG = 5
SCALE = HEAD_DIM ** -0.5 * 1.4426950408889634
LOW = -1e30


def kernel(groups, tok, wq, wk, wv, win, glob, fb, out, big, wbuf, qbuf, kbuf, vbuf, bias, bounds,
           part_own, part_pair, part_bnd, acc, top, ring_sem, side_sem, recv_sem, local_sem):
    seq = lax.axis_index("seq")
    head = lax.axis_index("head")
    group = seq // 4
    low = seq % 4
    half_id = head // 2
    core = head % 2
    y = half_id * 4 + low
    odd = low % 2
    sgn = 1 - 2 * odd
    h_f, h_b = odd, 1 - odd

    def slot_of(yy):
        return lax.rem(yy + 2 * RING, RING)

    def at(g, yy, c):
        yy = slot_of(yy)
        return (g * 4 + lax.rem(yy, 4), (yy // 4) * 2 + c)

    ahead, behind = at(group, y + sgn, core), at(group, y - sgn, core)
    mate = at(group, y, 1 - core)
    next_group = lax.rem(group + sgn + groups, groups)
    last_group = lax.rem(group - sgn + groups, groups)
    side = at(next_group, y, core)

    own_first = pl.multiple_of(seq * ROWS, ROWS)
    mine = pl.ds(pl.multiple_of(core * FEAT, FEAT), FEAT)
    theirs = pl.ds(pl.multiple_of((1 - core) * FEAT, FEAT), FEAT)
    load_tok = pltpu.make_async_copy(tok, big.at[y, :, mine], local_sem.at[0])
    load_fb = pltpu.make_async_copy(fb.at[:, pl.ds(own_first, ROWS)], bounds, local_sem.at[1])
    load_w = [
        pltpu.make_async_copy(w, wbuf.at[:, pl.ds(i * FEAT, FEAT)], local_sem.at[2 + i])
        for i, w in enumerate((wq, wk, wv))
    ]

    barrier = pltpu.get_barrier_semaphore()
    peers = (ahead, behind, mate, side, at(last_group, y, core))
    for peer in peers:
        pl.semaphore_signal(barrier, inc=1, device_id=peer, device_id_type=MESH)
    load_tok.start()
    load_fb.start()
    pl.semaphore_wait(barrier, len(peers))

    waits = []
    counts = {"ring": 0, "side": 0}

    def rows_of(half, k=None):
        if k is None:
            return pl.ds(pl.multiple_of(half * HALF, HALF), HALF)
        return pl.ds(pl.multiple_of(half * HALF + k * SUB, SUB), SUB)

    def send(kind, src_slot, dst_slot, half, k, target, own=False):
        rows = rows_of(half, k)
        to = dst_slot + (OTHER if target is mate else 0)
        copy = pltpu.make_async_remote_copy(
            src_ref=tok.at[rows] if own else big.at[src_slot, rows, mine],
            dst_ref=big.at[dst_slot, rows, mine],
            send_sem=(ring_sem if kind == "ring" else side_sem).at[counts[kind]],
            recv_sem=recv_sem.at[to, half * SUBS + (k or 0)],
            device_id=target,
            device_id_type=MESH,
        )
        copy.start()
        counts[kind] += 1
        waits.append(copy)

    def to_mate(slot, half, k=None, own=False):
        send("side", slot, slot, half, k, mate, own)

    def arrived(slot, half, k=None):
        ref = big.at[slot, rows_of(half, k), mine]
        pltpu.make_async_copy(ref, ref, recv_sem.at[slot, half * SUBS + (k or 0)]).wait()

    def mate_arrived(slot, half, k=None):
        ref = big.at[slot, rows_of(half, k), theirs]
        pltpu.make_async_copy(ref, ref, recv_sem.at[slot + OTHER, half * SUBS + (k or 0)]).wait()

    def step(s, pieces=range(SUBS)):
        f, b = slot_of(y - s * sgn), slot_of(y + s * sgn)
        for k in pieces:
            arrived(f, h_f, k)
            if s < LONG:
                send("ring", f, f, h_f, k, ahead)
            else:
                send("side", f, BND + 1, h_f, k, side)
            arrived(b, h_b, k)
            if s < LONG:
                send("ring", b, b, h_b, k, behind)
        if SUBS - 1 not in pieces:
            return
        if s == 1:
            send("side", f, BND, h_f, None, side)
        elif s in (3, 4):
            to_mate(f, h_f)
        if s == 3:
            send("side", b, BND + 1, h_b, None, side)
        elif s != 2:
            to_mate(b, h_b)

    def short_way(k):
        f, b = slot_of(y - sgn), slot_of(y + sgn)
        arrived(f, h_b, k)
        send("side", f, BND, h_b, k, side)
        arrived(b, h_f, k)
        if k == SUBS - 1:
            to_mate(b, h_f)

    def bnd_arrived(which, half, k=None):
        arrived(BND + which, half, k)
        to_mate(BND + which, half, k)

    g_near = half_id * 2
    g_far = 2 - g_near

    def product(slot, g, half, tile):
        w = wbuf[pl.ds(pl.multiple_of(g * FEAT, 2 * FEAT), 2 * FEAT), tile * FEAT:(tile + 1) * FEAT]
        return jnp.dot(big[slot, rows_of(half), :], w, preferred_element_type=jnp.float32)

    def first_part(part, slot, g, half, tiles):
        for i, tile in enumerate(tiles):
            part[rows_of(half), i * FEAT:(i + 1) * FEAT] = product(slot, g, half, tile)

    def second_part(part, slot, g, half, tiles, run):
        keys = pl.ds(pl.multiple_of(run * ROWS + half * HALF, HALF), HALF)
        for i, tile in enumerate(tiles):
            whole = part[rows_of(half), i * FEAT:(i + 1) * FEAT] + product(slot, g, half, tile)
            if tile == 0:
                qbuf[rows_of(half), :] = whole.astype(jnp.bfloat16)
            elif tile == 1:
                kbuf[keys, :] = whole.astype(jnp.bfloat16)
            else:
                for h in range(HEADS):
                    vbuf[h, 0:HEAD_DIM, keys] = whole[:, h * HEAD_DIM:(h + 1) * HEAD_DIM].T.astype(jnp.bfloat16)

    def make_bias():
        for e in range(12):
            blk = seq * 4 - 4 + e
            row = lax.broadcasted_iota(jnp.int32, (BLOCK, BLOCK), 0)
            for p in range(4):
                cols = slice(p * BLOCK, (p + 1) * BLOCK)
                me = seq * 4 + p
                ok = (abs(e - 4 - p) <= win[me]) | (glob[0, me] == blk) | (glob[1, me] == blk)
                pos = jnp.where(ok, blk * BLOCK, -(1 << 20)) + row
                keep = (pos >= bounds[0:1, cols]) & (pos < bounds[1:2, cols])
                bias[e * BLOCK:(e + 1) * BLOCK, cols] = jnp.where(keep, 0.0, -jnp.inf)

    def attend(run, first_key, keys, query_half=None, heads=range(HEADS)):
        k_rows = pl.ds(pl.multiple_of(run * ROWS + first_key, HALF), keys)
        q_rows = slice(None) if query_half is None else rows_of(query_half)
        mask = bias[k_rows, q_rows]
        for h in heads:
            hc = slice(h * HEAD_DIM, (h + 1) * HEAD_DIM)
            score = lax.dot_general(
                kbuf[k_rows, hc], qbuf[q_rows, hc], (((1,), (1,)), ((), ())), preferred_element_type=jnp.float32
            ) + mask
            old = top[h, :, q_rows]
            high = jnp.maximum(jnp.max(score, axis=0, keepdims=True), old)
            expo = jnp.exp2((score - high) * SCALE).astype(jnp.bfloat16)
            mixed = jnp.dot(vbuf[h, :, k_rows], expo, preferred_element_type=jnp.float32)
            acc[h, :, q_rows] = mixed + jnp.exp2((old - high) * SCALE) * acc[h, :, q_rows]
            top[h, :, q_rows] = high

    def finish(half):
        for h in range(HEADS):
            mean = acc[h, 0:HEAD_DIM, rows_of(half)] / acc[h, HEAD_DIM:HEAD_DIM + 1, rows_of(half)]
            out[rows_of(half), h * HEAD_DIM:(h + 1) * HEAD_DIM] = mean.T.astype(jnp.bfloat16)

    own_far = slot_of(y + 4)
    pair_near, pair_far = slot_of(y + sgn), slot_of(y - 3 * sgn)
    pair_run, bnd_run = 1 + sgn, 1 - sgn
    both, keyval = (0, 1), (1, 2)

    for k in range(SUBS):
        send("ring", y, y, h_f, k, ahead, True)
        send("ring", y, y, h_b, k, behind, True)
    for half in both:
        to_mate(y, half, None, True)
    for load in load_w:
        load.start()
    acc[...] = jnp.zeros_like(acc)
    top[...] = jnp.full_like(top, LOW)
    vbuf[:, HEAD_DIM:, :] = jnp.ones_like(vbuf[:, HEAD_DIM:, :])
    load_fb.wait()
    make_bias()
    load_tok.wait()
    step(1)
    for load in load_w:
        load.wait()
    mate_arrived(y, 0)
    first_part(part_own, y, g_near, 0, (0, 1, 2))
    step(2)
    mate_arrived(y, 1)
    first_part(part_own, y, g_near, 1, (0, 1, 2))
    step(3)
    for k in range(SUBS):
        send("ring", y, y, h_b, k, ahead, True)
        send("ring", y, y, h_f, k, behind, True)
    bnd_arrived(0, h_f)
    mate_arrived(pair_near, h_b)
    first_part(part_pair, pair_near, g_near, h_b, keyval)
    mate_arrived(BND, h_f)
    first_part(part_bnd, BND, g_far, h_f, keyval)
    mate_arrived(pair_far, h_f)
    first_part(part_pair, pair_far, g_far, h_f, keyval)
    step(4)
    short_way(0)
    mate_arrived(own_far, 0)
    second_part(part_own, own_far, g_far, 0, (0, 1, 2), 1)
    short_way(1)
    bnd_arrived(1, h_b)
    mate_arrived(own_far, 1)
    second_part(part_own, own_far, g_far, 1, (0, 1, 2), 1)
    short_way(2)
    attend(1, 0, ROWS, None, (0, 1))
    short_way(3)
    attend(1, 0, ROWS, None, (2, 3))
    step(5, (0,))
    mate_arrived(BND + 1, h_b)
    first_part(part_bnd, BND + 1, g_near, h_b, keyval)
    step(5, (1,))
    for k in range(SUBS):
        arrived(BND, h_b, k)
    to_mate(BND, h_b)
    mate_arrived(pair_near, h_f)
    second_part(part_pair, pair_near, g_near, h_f, keyval, pair_run)
    step(5, (2,))
    attend(pair_run, h_f * HALF, HALF)
    step(5, (3,))
    bnd_arrived(1, h_f, 0)
    mate_arrived(BND, h_b)
    second_part(part_bnd, BND, g_far, h_b, keyval, bnd_run)
    bnd_arrived(1, h_f, 1)
    attend(bnd_run, h_b * HALF, HALF)
    bnd_arrived(1, h_f, 2)
    mate_arrived(pair_far, h_b)
    second_part(part_pair, pair_far, g_far, h_b, keyval, pair_run)
    bnd_arrived(1, h_f, 3)
    attend(pair_run, h_b * HALF, HALF, h_b)
    finish(h_b)
    for k in range(SUBS):
        mate_arrived(BND + 1, h_f, k)
    second_part(part_bnd, BND + 1, g_near, h_f, keyval, bnd_run)
    attend(bnd_run, h_f * HALF, HALF, h_f)
    finish(h_f)
    for copy in waits:
        copy.wait_send()


def local(groups, tokens, w_query, w_key, w_value, window, global_blocks, file_bounds):
    anywhere = pl.BlockSpec(memory_space=pl.ANY)
    scalars = pl.BlockSpec(memory_space=pltpu.SMEM)
    return pl.pallas_call(
        functools.partial(kernel, groups),
        out_shape=pltpu.VMEM((ROWS, FEAT), jnp.bfloat16),
        in_specs=[anywhere] * 4 + [scalars] * 2 + [anywhere],
        out_specs=pl.BlockSpec(memory_space=pltpu.VMEM),
        scratch_shapes=[
            pltpu.VMEM((10, ROWS, 2 * FEAT), jnp.bfloat16),
            pltpu.VMEM((2048, 3 * FEAT), jnp.bfloat16),
            pltpu.VMEM((ROWS, FEAT), jnp.bfloat16),
            pltpu.VMEM((3 * ROWS, FEAT), jnp.bfloat16),
            pltpu.VMEM((HEADS, HEAD_DIM + 16, 3 * ROWS), jnp.bfloat16),
            pltpu.VMEM((3 * ROWS, ROWS), jnp.float32),
            pltpu.VMEM((2, ROWS), jnp.int32),
            pltpu.VMEM((ROWS, 3 * FEAT), jnp.float32),
            pltpu.VMEM((ROWS, 2 * FEAT), jnp.float32),
            pltpu.VMEM((ROWS, 2 * FEAT), jnp.float32),
            pltpu.VMEM((HEADS, HEAD_DIM + 16, ROWS), jnp.float32),
            pltpu.VMEM((HEADS, 1, ROWS), jnp.float32),
            pltpu.SemaphoreType.DMA((12 * SUBS,)),
            pltpu.SemaphoreType.DMA((13 + 3 * SUBS,)),
            pltpu.SemaphoreType.DMA((20, 2 * SUBS)),
            pltpu.SemaphoreType.DMA((5,)),
        ],
        compiler_params=pltpu.CompilerParams(
            collective_id=0, has_side_effects=True, vmem_limit_bytes=56 << 20
        ),
        cost_estimate=pl.CostEstimate(flops=9_000_000_000, bytes_accessed=8_000_000, transcendentals=3_000_000),
        name="gather_project_attend",
    )(tokens, w_query, w_key, w_value, window, global_blocks.T, file_bounds)


def solution(mesh):
    placed = (P("seq", "head"), P(None, "head"), P(None, "head"), P(None, "head"), P(), P(), P())
    return jax.shard_map(
        functools.partial(local, mesh.shape["seq"] // 4),
        mesh=mesh, in_specs=placed, out_specs=P("seq", "head"), check_vma=False,
    )
```

```python
import functools

import jax
import jax.numpy as jnp
from jax import lax
from jax.experimental import pallas as pl
from jax.experimental.pallas import tpu as pltpu
from jax.sharding import PartitionSpec as P

MESH = pl.DeviceIdType.MESH
HEAD_DIM = 128
BLOCK = 128
ROWS = 512
FEAT = 512
HALF = 256
RING = 8
HEADS = 4
SUBS = 4
SUB = HALF // SUBS
BND = 8
TMP = 10
OTHER = 11
LONG = 5
SCALE = HEAD_DIM ** -0.5 * 1.4426950408889634
LOW = -1e30


def kernel(groups, tok, wq, wk, wv, win, glob, fb, out, big, wbuf, qbuf, kbuf, vbuf, bias, bounds,
           part_own, part_pair, part_bnd, acc, top, ring_sem, side_sem, recv_sem, local_sem):
    seq = lax.axis_index("seq")
    head = lax.axis_index("head")
    group = seq // 4
    low = seq % 4
    half_id = head // 2
    core = head % 2
    y = half_id * 4 + low
    odd = low % 2
    sgn = 1 - 2 * odd
    h_f, h_b = odd, 1 - odd

    def slot_of(yy):
        return lax.rem(yy + 2 * RING, RING)

    def at(g, yy, c):
        yy = slot_of(yy)
        return (g * 4 + lax.rem(yy, 4), (yy // 4) * 2 + c)

    ahead, behind = at(group, y + sgn, core), at(group, y - sgn, core)
    mate = at(group, y, 1 - core)
    next_group = lax.rem(group + sgn + groups, groups)
    last_group = lax.rem(group - sgn + groups, groups)
    side, back_side = at(next_group, y, core), at(last_group, y, core)

    own_first = pl.multiple_of(seq * ROWS, ROWS)
    mine = pl.ds(pl.multiple_of(core * FEAT, FEAT), FEAT)
    theirs = pl.ds(pl.multiple_of((1 - core) * FEAT, FEAT), FEAT)
    load_tok = pltpu.make_async_copy(tok, big.at[y, :, mine], local_sem.at[0])
    load_fb = pltpu.make_async_copy(fb.at[:, pl.ds(own_first, ROWS)], bounds, local_sem.at[1])
    load_w = [
        pltpu.make_async_copy(w, wbuf.at[:, pl.ds(i * FEAT, FEAT)], local_sem.at[2 + i])
        for i, w in enumerate((wq, wk, wv))
    ]

    barrier = pltpu.get_barrier_semaphore()
    peers = (ahead, behind, mate, side, back_side)
    for peer in peers:
        pl.semaphore_signal(barrier, inc=1, device_id=peer, device_id_type=MESH)
    load_tok.start()
    load_fb.start()
    pl.semaphore_wait(barrier, len(peers))

    waits = []
    counts = {"ring": 0, "side": 0}

    def rows_of(half, k=None):
        if k is None:
            return pl.ds(pl.multiple_of(half * HALF, HALF), HALF)
        return pl.ds(pl.multiple_of(half * HALF + k * SUB, SUB), SUB)

    def send(kind, src_slot, dst_slot, half, k, target, own=False):
        rows = rows_of(half, k)
        to = dst_slot + (OTHER if target is mate else 0)
        copy = pltpu.make_async_remote_copy(
            src_ref=tok.at[rows] if own else big.at[src_slot, rows, mine],
            dst_ref=big.at[dst_slot, rows, mine],
            send_sem=(ring_sem if kind == "ring" else side_sem).at[counts[kind]],
            recv_sem=recv_sem.at[to, half * SUBS + (k or 0)],
            device_id=target,
            device_id_type=MESH,
        )
        copy.start()
        counts[kind] += 1
        waits.append(copy)

    def to_mate(slot, half, k=None, own=False):
        send("side", slot, slot, half, k, mate, own)

    def arrived(slot, half, k=None):
        ref = big.at[slot, rows_of(half, k), mine]
        pltpu.make_async_copy(ref, ref, recv_sem.at[slot, half * SUBS + (k or 0)]).wait()

    def mate_arrived(slot, half, k=None):
        ref = big.at[slot, rows_of(half, k), theirs]
        pltpu.make_async_copy(ref, ref, recv_sem.at[slot + OTHER, half * SUBS + (k or 0)]).wait()

    def step(s):
        f, b = slot_of(y - s * sgn), slot_of(y + s * sgn)
        for k in range(SUBS):
            arrived(f, h_f, k)
            send("ring", f, f, h_f, k, ahead)
            arrived(b, h_b, k)
            if s < LONG - 1:
                send("ring", b, b, h_b, k, behind)
            else:
                send("side", b, TMP, h_b, k, back_side)
        if s == 1:
            send("side", f, BND, h_f, None, side)
        elif s in (3, 4):
            to_mate(f, h_f)
        if s == 3:
            send("side", b, BND + 1, h_b, None, side)
        elif s != 2:
            to_mate(b, h_b)

    def pass_on(k):
        arrived(TMP, h_b, k)
        send("ring", TMP, BND + 1, h_b, k, behind)

    def short_way():
        for k in range(SUBS):
            arrived(BND, h_b, k)
            arrived(pair_near, h_f, k)
        to_mate(BND, h_b)
        to_mate(pair_near, h_f)

    def last(k):
        bnd_arrived(1, h_f, k)
        arrived(pair_far, h_b, k)
        to_mate(pair_far, h_b, k)

    def bnd_arrived(which, half, k=None):
        arrived(BND + which, half, k)
        to_mate(BND + which, half, k)

    own_far = slot_of(y + 4)
    pair_near, pair_far = slot_of(y + sgn), slot_of(y - 3 * sgn)
    g_near = half_id * 2
    g_far = 2 - g_near

    def product(slot, g, half, tile):
        w = wbuf[pl.ds(pl.multiple_of(g * FEAT, 2 * FEAT), 2 * FEAT), tile * FEAT:(tile + 1) * FEAT]
        return jnp.dot(big[slot, rows_of(half), :], w, preferred_element_type=jnp.float32)

    def first_part(part, slot, g, half, tiles):
        for i, tile in enumerate(tiles):
            part[rows_of(half), i * FEAT:(i + 1) * FEAT] = product(slot, g, half, tile)

    def second_part(part, slot, g, half, tiles, run):
        keys = pl.ds(pl.multiple_of(run * ROWS + half * HALF, HALF), HALF)
        for i, tile in enumerate(tiles):
            whole = part[rows_of(half), i * FEAT:(i + 1) * FEAT] + product(slot, g, half, tile)
            if tile == 0:
                qbuf[rows_of(half), :] = whole.astype(jnp.bfloat16)
            elif tile == 1:
                kbuf[keys, :] = whole.astype(jnp.bfloat16)
            else:
                for h in range(HEADS):
                    vbuf[h, 0:HEAD_DIM, keys] = whole[:, h * HEAD_DIM:(h + 1) * HEAD_DIM].T.astype(jnp.bfloat16)

    def make_bias():
        for e in range(12):
            blk = seq * 4 - 4 + e
            row = lax.broadcasted_iota(jnp.int32, (BLOCK, BLOCK), 0)
            for p in range(4):
                cols = slice(p * BLOCK, (p + 1) * BLOCK)
                me = seq * 4 + p
                ok = (abs(e - 4 - p) <= win[me]) | (glob[0, me] == blk) | (glob[1, me] == blk)
                pos = jnp.where(ok, blk * BLOCK, -(1 << 20)) + row
                keep = (pos >= bounds[0:1, cols]) & (pos < bounds[1:2, cols])
                bias[e * BLOCK:(e + 1) * BLOCK, cols] = jnp.where(keep, 0.0, -jnp.inf)

    def attend(run, first_key, keys, query_half=None, heads=range(HEADS)):
        k_rows = pl.ds(pl.multiple_of(run * ROWS + first_key, HALF), keys)
        q_rows = slice(None) if query_half is None else rows_of(query_half)
        mask = bias[k_rows, q_rows]
        for h in heads:
            hc = slice(h * HEAD_DIM, (h + 1) * HEAD_DIM)
            score = lax.dot_general(
                kbuf[k_rows, hc], qbuf[q_rows, hc], (((1,), (1,)), ((), ())), preferred_element_type=jnp.float32
            ) + mask
            old = top[h, :, q_rows]
            high = jnp.maximum(jnp.max(score, axis=0, keepdims=True), old)
            expo = jnp.exp2((score - high) * SCALE).astype(jnp.bfloat16)
            mixed = jnp.dot(vbuf[h, :, k_rows], expo, preferred_element_type=jnp.float32)
            acc[h, :, q_rows] = mixed + jnp.exp2((old - high) * SCALE) * acc[h, :, q_rows]
            top[h, :, q_rows] = high

    def finish(half):
        for h in range(HEADS):
            mean = acc[h, 0:HEAD_DIM, rows_of(half)] / acc[h, HEAD_DIM:HEAD_DIM + 1, rows_of(half)]
            out[rows_of(half), h * HEAD_DIM:(h + 1) * HEAD_DIM] = mean.T.astype(jnp.bfloat16)

    pair_run, bnd_run = 1 + sgn, 1 - sgn
    both, keyval = (0, 1), (1, 2)

    for k in range(SUBS):
        send("ring", y, y, h_f, k, ahead, True)
        send("ring", y, y, h_b, k, behind, True)
    for half in both:
        to_mate(y, half, None, True)
    send("side", y, TMP, h_f, None, back_side, True)
    for load in load_w:
        load.start()
    acc[...] = jnp.zeros_like(acc)
    top[...] = jnp.full_like(top, LOW)
    vbuf[:, HEAD_DIM:, :] = jnp.ones_like(vbuf[:, HEAD_DIM:, :])
    load_fb.wait()
    make_bias()
    load_tok.wait()
    step(1)
    for load in load_w:
        load.wait()
    mate_arrived(y, 0)
    first_part(part_own, y, g_near, 0, (0, 1, 2))
    step(2)
    mate_arrived(y, 1)
    first_part(part_own, y, g_near, 1, (0, 1, 2))
    step(3)
    arrived(TMP, h_f)
    for k in range(SUBS):
        send("ring", y, y, h_b, k, ahead, True)
        send("ring", TMP, BND, h_f, k, behind)
    bnd_arrived(0, h_f)
    mate_arrived(pair_near, h_b)
    first_part(part_pair, pair_near, g_near, h_b, keyval)
    mate_arrived(BND, h_f)
    first_part(part_bnd, BND, g_far, h_f, keyval)
    mate_arrived(pair_far, h_f)
    first_part(part_pair, pair_far, g_far, h_f, keyval)
    step(4)
    pass_on(0)
    pass_on(1)
    mate_arrived(own_far, 0)
    second_part(part_own, own_far, g_far, 0, (0, 1, 2), 1)
    pass_on(2)
    bnd_arrived(1, h_b)
    mate_arrived(own_far, 1)
    second_part(part_own, own_far, g_far, 1, (0, 1, 2), 1)
    pass_on(3)
    attend(1, 0, ROWS, None, (0, 1))
    short_way()
    attend(1, 0, ROWS, None, (2, 3))
    mate_arrived(BND + 1, h_b)
    first_part(part_bnd, BND + 1, g_near, h_b, keyval)
    last(0)
    mate_arrived(pair_near, h_f)
    second_part(part_pair, pair_near, g_near, h_f, keyval, pair_run)
    last(1)
    attend(pair_run, h_f * HALF, HALF)
    last(2)
    mate_arrived(BND, h_b)
    second_part(part_bnd, BND, g_far, h_b, keyval, bnd_run)
    last(3)
    attend(bnd_run, h_b * HALF, HALF)
    for k in range(SUBS):
        mate_arrived(pair_far, h_b, k)
    second_part(part_pair, pair_far, g_far, h_b, keyval, pair_run)
    attend(pair_run, h_b * HALF, HALF, h_b)
    finish(h_b)
    for k in range(SUBS):
        mate_arrived(BND + 1, h_f, k)
    second_part(part_bnd, BND + 1, g_near, h_f, keyval, bnd_run)
    attend(bnd_run, h_f * HALF, HALF, h_f)
    finish(h_f)
    for copy in waits:
        copy.wait_send()


def local(groups, tokens, w_query, w_key, w_value, window, global_blocks, file_bounds):
    anywhere = pl.BlockSpec(memory_space=pl.ANY)
    scalars = pl.BlockSpec(memory_space=pltpu.SMEM)
    return pl.pallas_call(
        functools.partial(kernel, groups),
        out_shape=pltpu.VMEM((ROWS, FEAT), jnp.bfloat16),
        in_specs=[anywhere] * 4 + [scalars] * 2 + [anywhere],
        out_specs=pl.BlockSpec(memory_space=pltpu.VMEM),
        scratch_shapes=[
            pltpu.VMEM((11, ROWS, 2 * FEAT), jnp.bfloat16),
            pltpu.VMEM((2048, 3 * FEAT), jnp.bfloat16),
            pltpu.VMEM((ROWS, FEAT), jnp.bfloat16),
            pltpu.VMEM((3 * ROWS, FEAT), jnp.bfloat16),
            pltpu.VMEM((HEADS, HEAD_DIM + 16, 3 * ROWS), jnp.bfloat16),
            pltpu.VMEM((3 * ROWS, ROWS), jnp.float32),
            pltpu.VMEM((2, ROWS), jnp.int32),
            pltpu.VMEM((ROWS, 3 * FEAT), jnp.float32),
            pltpu.VMEM((ROWS, 2 * FEAT), jnp.float32),
            pltpu.VMEM((ROWS, 2 * FEAT), jnp.float32),
            pltpu.VMEM((HEADS, HEAD_DIM + 16, ROWS), jnp.float32),
            pltpu.VMEM((HEADS, 1, ROWS), jnp.float32),
            pltpu.SemaphoreType.DMA((12 * SUBS,)),
            pltpu.SemaphoreType.DMA((13 + 3 * SUBS,)),
            pltpu.SemaphoreType.DMA((22, 2 * SUBS)),
            pltpu.SemaphoreType.DMA((5,)),
        ],
        compiler_params=pltpu.CompilerParams(
            collective_id=0, has_side_effects=True, vmem_limit_bytes=56 << 20
        ),
        cost_estimate=pl.CostEstimate(flops=9_000_000_000, bytes_accessed=8_000_000, transcendentals=3_000_000),
        name="gather_project_attend",
    )(tokens, w_query, w_key, w_value, window, global_blocks.T, file_bounds)


def solution(mesh):
    placed = (P("seq", "head"), P(None, "head"), P(None, "head"), P(None, "head"), P(), P(), P())
    return jax.shard_map(
        functools.partial(local, mesh.shape["seq"] // 4),
        mesh=mesh, in_specs=placed, out_specs=P("seq", "head"), check_vma=False,
    )
```

```python
import functools

import jax
import jax.numpy as jnp
from jax import lax
from jax.experimental import pallas as pl
from jax.experimental.pallas import tpu as pltpu
from jax.sharding import PartitionSpec as P

MESH = pl.DeviceIdType.MESH
HEAD_DIM = 128
BLOCK = 128
ROWS = 512
FEAT = 512
HALF = 256
RING = 8
HEADS = 4
SUBS = 4
SUB = HALF // SUBS
BND = 8
TMP = 10
OTHER = 11
LONG = 5
SCALE = HEAD_DIM ** -0.5 * 1.4426950408889634
LOW = -1e30


def kernel(groups, tok, wq, wk, wv, win, glob, fb, out, big, wbuf, qbuf, kbuf, vbuf, bias, bounds,
           part_own, part_pair, part_bnd, acc, top, ring_sem, side_sem, recv_sem, local_sem):
    seq = lax.axis_index("seq")
    head = lax.axis_index("head")
    group = seq // 4
    low = seq % 4
    half_id = head // 2
    core = head % 2
    y = half_id * 4 + low
    odd = low % 2
    sgn = 1 - 2 * odd
    h_f, h_b = odd, 1 - odd

    def slot_of(yy):
        return lax.rem(yy + 2 * RING, RING)

    def at(g, yy, c):
        yy = slot_of(yy)
        return (g * 4 + lax.rem(yy, 4), (yy // 4) * 2 + c)

    ahead, behind = at(group, y + sgn, core), at(group, y - sgn, core)
    mate = at(group, y, 1 - core)
    next_group = lax.rem(group + sgn + groups, groups)
    last_group = lax.rem(group - sgn + groups, groups)
    side, back_side = at(next_group, y, core), at(last_group, y, core)

    own_first = pl.multiple_of(seq * ROWS, ROWS)
    mine = pl.ds(pl.multiple_of(core * FEAT, FEAT), FEAT)
    theirs = pl.ds(pl.multiple_of((1 - core) * FEAT, FEAT), FEAT)
    load_tok = pltpu.make_async_copy(tok, big.at[y, :, mine], local_sem.at[0])
    load_fb = pltpu.make_async_copy(fb.at[:, pl.ds(own_first, ROWS)], bounds, local_sem.at[1])
    load_w = [
        pltpu.make_async_copy(w, wbuf.at[:, pl.ds(i * FEAT, FEAT)], local_sem.at[2 + i])
        for i, w in enumerate((wq, wk, wv))
    ]

    barrier = pltpu.get_barrier_semaphore()
    peers = (ahead, behind, mate, side, back_side)
    for peer in peers:
        pl.semaphore_signal(barrier, inc=1, device_id=peer, device_id_type=MESH)
    load_tok.start()
    load_fb.start()
    pl.semaphore_wait(barrier, len(peers))

    waits = []
    counts = {"ring": 0, "side": 0}

    def rows_of(half, k=None):
        if k is None:
            return pl.ds(pl.multiple_of(half * HALF, HALF), HALF)
        return pl.ds(pl.multiple_of(half * HALF + k * SUB, SUB), SUB)

    def send(kind, src_slot, dst_slot, half, k, target, own=False):
        rows = rows_of(half, k)
        to = dst_slot + (OTHER if target is mate else 0)
        copy = pltpu.make_async_remote_copy(
            src_ref=tok.at[rows] if own else big.at[src_slot, rows, mine],
            dst_ref=big.at[dst_slot, rows, mine],
            send_sem=(ring_sem if kind == "ring" else side_sem).at[counts[kind]],
            recv_sem=recv_sem.at[to, half * SUBS + (k or 0)],
            device_id=target,
            device_id_type=MESH,
        )
        copy.start()
        counts[kind] += 1
        waits.append(copy)

    def to_mate(slot, half, k=None, own=False):
        send("side", slot, slot, half, k, mate, own)

    def arrived(slot, half, k=None):
        ref = big.at[slot, rows_of(half, k), mine]
        pltpu.make_async_copy(ref, ref, recv_sem.at[slot, half * SUBS + (k or 0)]).wait()

    def mate_arrived(slot, half, k=None):
        ref = big.at[slot, rows_of(half, k), theirs]
        pltpu.make_async_copy(ref, ref, recv_sem.at[slot + OTHER, half * SUBS + (k or 0)]).wait()

    def step(s):
        f, b = slot_of(y - s * sgn), slot_of(y + s * sgn)
        for k in range(SUBS):
            arrived(f, h_f, k)
            send("ring", f, f, h_f, k, ahead)
            arrived(b, h_b, k)
            if s < LONG - 1:
                send("ring", b, b, h_b, k, behind)
            else:
                send("side", b, TMP, h_b, k, back_side)
        if s == 1:
            send("side", f, BND, h_f, None, side)
        elif s in (3, 4):
            to_mate(f, h_f)
        if s == 3:
            send("side", b, BND + 1, h_b, None, side)
        elif s != 2:
            to_mate(b, h_b)

    def pass_on(k):
        arrived(TMP, h_b, k)
        send("ring", TMP, BND + 1, h_b, k, behind)

    def short_way():
        for k in range(SUBS):
            arrived(BND, h_b, k)
            arrived(pair_near, h_f, k)
        to_mate(BND, h_b)
        to_mate(pair_near, h_f)

    def last(k):
        bnd_arrived(1, h_f, k)
        arrived(pair_far, h_b, k)
        to_mate(pair_far, h_b, k)

    def bnd_arrived(which, half, k=None):
        arrived(BND + which, half, k)
        to_mate(BND + which, half, k)

    own_far = slot_of(y + 4)
    pair_near, pair_far = slot_of(y + sgn), slot_of(y - 3 * sgn)
    g_near = half_id * 2
    g_far = 2 - g_near

    def product(slot, g, half, tile):
        w = wbuf[pl.ds(pl.multiple_of(g * FEAT, 2 * FEAT), 2 * FEAT), tile * FEAT:(tile + 1) * FEAT]
        return jnp.dot(big[slot, rows_of(half), :], w, preferred_element_type=jnp.float32)

    def first_part(part, slot, g, half, tiles):
        for i, tile in enumerate(tiles):
            part[rows_of(half), i * FEAT:(i + 1) * FEAT] = product(slot, g, half, tile)

    def second_part(part, slot, g, half, tiles, run):
        keys = pl.ds(pl.multiple_of(run * ROWS + half * HALF, HALF), HALF)
        for i, tile in enumerate(tiles):
            whole = part[rows_of(half), i * FEAT:(i + 1) * FEAT] + product(slot, g, half, tile)
            if tile == 0:
                qbuf[rows_of(half), :] = whole.astype(jnp.bfloat16)
            elif tile == 1:
                kbuf[keys, :] = whole.astype(jnp.bfloat16)
            else:
                for h in range(HEADS):
                    vbuf[h, 0:HEAD_DIM, keys] = whole[:, h * HEAD_DIM:(h + 1) * HEAD_DIM].T.astype(jnp.bfloat16)

    def make_bias():
        for e in range(12):
            blk = seq * 4 - 4 + e
            row = lax.broadcasted_iota(jnp.int32, (BLOCK, BLOCK), 0)
            for p in range(4):
                cols = slice(p * BLOCK, (p + 1) * BLOCK)
                me = seq * 4 + p
                ok = (abs(e - 4 - p) <= win[me]) | (glob[0, me] == blk) | (glob[1, me] == blk)
                pos = jnp.where(ok, blk * BLOCK, -(1 << 20)) + row
                keep = (pos >= bounds[0:1, cols]) & (pos < bounds[1:2, cols])
                bias[e * BLOCK:(e + 1) * BLOCK, cols] = jnp.where(keep, 0.0, -jnp.inf)

    def attend(run, first_key, keys, query_half=None, heads=range(HEADS)):
        k_rows = pl.ds(pl.multiple_of(run * ROWS + first_key, HALF), keys)
        q_rows = slice(None) if query_half is None else rows_of(query_half)
        mask = bias[k_rows, q_rows]
        for h in heads:
            hc = slice(h * HEAD_DIM, (h + 1) * HEAD_DIM)
            score = lax.dot_general(
                kbuf[k_rows, hc], qbuf[q_rows, hc], (((1,), (1,)), ((), ())), preferred_element_type=jnp.float32
            ) + mask
            old = top[h, :, q_rows]
            high = jnp.maximum(jnp.max(score, axis=0, keepdims=True), old)
            expo = jnp.exp2((score - high) * SCALE).astype(jnp.bfloat16)
            mixed = jnp.dot(vbuf[h, :, k_rows], expo, preferred_element_type=jnp.float32)
            acc[h, :, q_rows] = mixed + jnp.exp2((old - high) * SCALE) * acc[h, :, q_rows]
            top[h, :, q_rows] = high

    def finish(half):
        for h in range(HEADS):
            mean = acc[h, 0:HEAD_DIM, rows_of(half)] * (1.0 / acc[h, HEAD_DIM:HEAD_DIM + 1, rows_of(half)])
            out[rows_of(half), h * HEAD_DIM:(h + 1) * HEAD_DIM] = mean.T.astype(jnp.bfloat16)

    pair_run, bnd_run = 1 + sgn, 1 - sgn
    both, keyval = (0, 1), (1, 2)

    for k in range(SUBS):
        send("ring", y, y, h_f, k, ahead, True)
        send("ring", y, y, h_b, k, behind, True)
    for half in both:
        to_mate(y, half, None, True)
    send("side", y, TMP, h_f, None, back_side, True)
    for load in load_w:
        load.start()
    acc[...] = jnp.zeros_like(acc)
    top[...] = jnp.full_like(top, LOW)
    vbuf[:, HEAD_DIM:, :] = jnp.ones_like(vbuf[:, HEAD_DIM:, :])
    load_fb.wait()
    make_bias()
    load_tok.wait()
    step(1)
    for load in load_w:
        load.wait()
    mate_arrived(y, 0)
    first_part(part_own, y, g_near, 0, (0, 1, 2))
    step(2)
    mate_arrived(y, 1)
    first_part(part_own, y, g_near, 1, (0, 1, 2))
    step(3)
    arrived(TMP, h_f)
    for k in range(SUBS):
        send("ring", y, y, h_b, k, ahead, True)
        send("ring", TMP, BND, h_f, k, behind)
    bnd_arrived(0, h_f)
    mate_arrived(pair_near, h_b)
    first_part(part_pair, pair_near, g_near, h_b, keyval)
    mate_arrived(BND, h_f)
    first_part(part_bnd, BND, g_far, h_f, keyval)
    mate_arrived(pair_far, h_f)
    first_part(part_pair, pair_far, g_far, h_f, keyval)
    step(4)
    pass_on(0)
    pass_on(1)
    mate_arrived(own_far, 0)
    second_part(part_own, own_far, g_far, 0, (0, 1, 2), 1)
    pass_on(2)
    bnd_arrived(1, h_b)
    mate_arrived(own_far, 1)
    second_part(part_own, own_far, g_far, 1, (0, 1, 2), 1)
    pass_on(3)
    attend(1, 0, ROWS)
    short_way()
    mate_arrived(BND + 1, h_b)
    first_part(part_bnd, BND + 1, g_near, h_b, keyval)
    last(0)
    mate_arrived(pair_near, h_f)
    second_part(part_pair, pair_near, g_near, h_f, keyval, pair_run)
    last(1)
    attend(pair_run, h_f * HALF, HALF)
    last(2)
    mate_arrived(BND, h_b)
    second_part(part_bnd, BND, g_far, h_b, keyval, bnd_run)
    attend(bnd_run, h_b * HALF, HALF, None, (0, 1))
    last(3)
    attend(bnd_run, h_b * HALF, HALF, None, (2, 3))
    for k in range(SUBS):
        mate_arrived(pair_far, h_b, k)
    second_part(part_pair, pair_far, g_far, h_b, keyval, pair_run)
    attend(pair_run, h_b * HALF, HALF, h_b)
    finish(h_b)
    for k in range(SUBS):
        mate_arrived(BND + 1, h_f, k)
    second_part(part_bnd, BND + 1, g_near, h_f, keyval, bnd_run)
    attend(bnd_run, h_f * HALF, HALF, h_f)
    finish(h_f)
    for copy in waits:
        copy.wait_send()


def local(groups, tokens, w_query, w_key, w_value, window, global_blocks, file_bounds):
    anywhere = pl.BlockSpec(memory_space=pl.ANY)
    scalars = pl.BlockSpec(memory_space=pltpu.SMEM)
    return pl.pallas_call(
        functools.partial(kernel, groups),
        out_shape=pltpu.VMEM((ROWS, FEAT), jnp.bfloat16),
        in_specs=[anywhere] * 4 + [scalars] * 2 + [anywhere],
        out_specs=pl.BlockSpec(memory_space=pltpu.VMEM),
        scratch_shapes=[
            pltpu.VMEM((11, ROWS, 2 * FEAT), jnp.bfloat16),
            pltpu.VMEM((2048, 3 * FEAT), jnp.bfloat16),
            pltpu.VMEM((ROWS, FEAT), jnp.bfloat16),
            pltpu.VMEM((3 * ROWS, FEAT), jnp.bfloat16),
            pltpu.VMEM((HEADS, HEAD_DIM + 16, 3 * ROWS), jnp.bfloat16),
            pltpu.VMEM((3 * ROWS, ROWS), jnp.float32),
            pltpu.VMEM((2, ROWS), jnp.int32),
            pltpu.VMEM((ROWS, 3 * FEAT), jnp.float32),
            pltpu.VMEM((ROWS, 2 * FEAT), jnp.float32),
            pltpu.VMEM((ROWS, 2 * FEAT), jnp.float32),
            pltpu.VMEM((HEADS, HEAD_DIM + 16, ROWS), jnp.float32),
            pltpu.VMEM((HEADS, 1, ROWS), jnp.float32),
            pltpu.SemaphoreType.DMA((12 * SUBS,)),
            pltpu.SemaphoreType.DMA((13 + 3 * SUBS,)),
            pltpu.SemaphoreType.DMA((22, 2 * SUBS)),
            pltpu.SemaphoreType.DMA((5,)),
        ],
        compiler_params=pltpu.CompilerParams(
            collective_id=0, has_side_effects=True, vmem_limit_bytes=56 << 20
        ),
        cost_estimate=pl.CostEstimate(flops=9_000_000_000, bytes_accessed=8_000_000, transcendentals=3_000_000),
        name="gather_project_attend",
    )(tokens, w_query, w_key, w_value, window, global_blocks.T, file_bounds)


def solution(mesh):
    placed = (P("seq", "head"), P(None, "head"), P(None, "head"), P(None, "head"), P(), P(), P())
    return jax.shard_map(
        functools.partial(local, mesh.shape["seq"] // 4),
        mesh=mesh, in_specs=placed, out_specs=P("seq", "head"), check_vma=False,
    )
```
